32 devices in a mesh: groups: 2 (over y), loop: 16 (over z, x, core).
Axes of the slice: x: 2, y: 2, z: 4, core: 2. Of those that a mesh axis runs over, the one named last changes fastest.
Arguments:
- image_feats: bfloat16 [4096, 768], P(('groups', 'loop')), parts along dimension 0, may hold values from -4 to 4
- text_feats: bfloat16 [4096, 768], P(('groups', 'loop')), parts along dimension 0, may hold values from -4 to 4
- image_proj: bfloat16 [768, 256], replicated, may hold values from -0.12629537 to 0.12629537
- text_proj: bfloat16 [768, 256], replicated, may hold values from -0.12629537 to 0.12629537
- pair_ids: int32 [4096], P(('groups', 'loop')), parts along dimension 0, may hold values from 0 to 255
- log_temp: float32 [1], replicated, may hold values from 2.7 to 3
- bias: float32 [1], replicated, may hold values from -7 to -5.5
- loss_grad: float32 [1], replicated, may hold values from 8 to 24
Outputs:
- image_grad: bfloat16 [4096, 768], P(('groups', 'loop')), parts along dimension 0
- text_grad: bfloat16 [4096, 768], P(('groups', 'loop')), parts along dimension 0
- weight_grads: float32 [1536, 512], P(('groups', 'loop')), parts along dimension 0
The draws below stay inside these ranges and needn't reach their ends.
There are 2 independent parts, one for each index of `groups`. The reference program is written for one: setup_inputs(seed, part) draws one part's arguments, and reference() takes and returns one part's arrays. A program takes and returns all parts, laid end to end along the dimension named above; an argument that names none is the same for every part. Nothing has to cross between parts.
All inputs are finite; a program needn't handle non-finite values.
Results may differ from the reference program's by a relative error of at most 0.0062.
Values may be sent and summed in bfloat16 or wider, within the bound.
A program may use at most 64 MiB of HBM per device.

```python
import math
import jax
import jax.numpy as jnp
from jax import lax

E = 768
P_SIZE = 256
N = 2048


def pair_labels(key):
    labels = jax.random.randint(jax.random.fold_in(key, 10), (N,), 0, N // 8, dtype=jnp.int32)
    marked = jax.random.randint(jax.random.fold_in(key, 11), (), 0, N, dtype=jnp.int32)
    places = jnp.arange(N, dtype=jnp.int32)
    labels = jnp.where(places == marked, N // 8 - 1, labels)
    labels = jnp.where(places == (marked + N // 2) % N, 0, labels)
    return labels


def pair_latent(key):
    labels = pair_labels(key)
    latent_rows = jax.random.normal(jax.random.fold_in(key, 12), (N // 8, E), jnp.float32)
    return jnp.take(latent_rows, labels, axis=0)


def head_common(key):
    return jax.random.normal(jax.random.fold_in(key, 40), (E, P_SIZE), jnp.float32)


def draw_pair_ids(key, part):
    labels = pair_labels(key)
    return labels


def draw_image_feats(key, part):
    latent = pair_latent(key)
    key = jax.random.fold_in(key, 4)
    spread = jax.random.normal(key, (N, E), jnp.float32)
    return jnp.clip((latent + 0.8 * spread) / math.sqrt(1.64), -4.0, 4.0).astype(jnp.bfloat16)


def draw_text_feats(key, part):
    latent = pair_latent(key)
    key = jax.random.fold_in(key, 5)
    spread = jax.random.normal(key, (N, E), jnp.float32)
    return jnp.clip((latent + 0.8 * spread) / math.sqrt(1.64), -4.0, 4.0).astype(jnp.bfloat16)


def draw_image_proj(key, part):
    common = head_common(key)
    key = jax.random.fold_in(key, 6)
    own_part = jax.random.normal(key, (E, P_SIZE), jnp.float32)
    mixed = jnp.clip((common + 0.5 * own_part) / math.sqrt(1.25), -3.5, 3.5)
    return (mixed / math.sqrt(E)).astype(jnp.bfloat16)


def draw_text_proj(key, part):
    common = head_common(key)
    key = jax.random.fold_in(key, 7)
    own_part = jax.random.normal(key, (E, P_SIZE), jnp.float32)
    mixed = jnp.clip((common + 0.5 * own_part) / math.sqrt(1.25), -3.5, 3.5)
    return (mixed / math.sqrt(E)).astype(jnp.bfloat16)


def setup_inputs(seed: int = 0, part: int = 0) -> dict:
    key_list = jax.random.split(jax.random.key(seed), 9)
    part_splits = jax.random.split(jax.random.fold_in(key_list[8], part), 9)
    return {
        "image_feats": draw_image_feats(jax.random.fold_in(jax.random.fold_in(key_list[8], part), 71), part),
        "text_feats": draw_text_feats(jax.random.fold_in(jax.random.fold_in(key_list[8], part), 71), part),
        "image_proj": draw_image_proj(jax.random.fold_in(key_list[8], 71), part),
        "text_proj": draw_text_proj(jax.random.fold_in(key_list[8], 71), part),
        "pair_ids": draw_pair_ids(jax.random.fold_in(jax.random.fold_in(key_list[8], part), 71), part),
        "log_temp": jnp.clip(jax.random.uniform(key_list[5], (1,), jnp.float32, 2.7, 3.0), 2.7, 3.0),
        "bias": jnp.clip(jax.random.uniform(key_list[6], (1,), jnp.float32, -7.0, -5.5), -7.0, -5.5),
        "loss_grad": jnp.clip(jnp.exp(jax.random.uniform(key_list[7], (1,), jnp.float32, math.log(8.0), math.log(24.0))), 8.0, 24.0),
    }


def unit_rows(raw):
    norm = jnp.sqrt(lax.optimization_barrier(jnp.sum(raw * raw, axis=-1, keepdims=True)) + 1e-06)
    return (raw / norm, norm)

def side_grad(own_half, other_half, ids_all, temp, bias_v, scale):
    rows = math.gcd(N, 512)
    own_blocks = own_half.reshape(N // rows, rows, own_half.shape[1])
    id_blocks = ids_all.reshape(N // rows, rows)

    def one_block(pair):
        block, block_ids = pair
        logits = temp * jnp.dot(block, other_half.T, preferred_element_type=jnp.float32) + bias_v
        equal = (block_ids[:, None] == ids_all[None, :]).astype(jnp.float32)
        coeff = (scale * (jax.nn.sigmoid(logits) - equal)).astype(jnp.bfloat16)
        return temp * jnp.dot(coeff, other_half, preferred_element_type=jnp.float32)
    result = lax.map(one_block, (own_blocks, id_blocks))
    return result.reshape(N, other_half.shape[1])

def reference(image_feats, text_feats, image_proj, text_proj, pair_ids, log_temp, bias, loss_grad):
    image_raw = jnp.dot(image_feats, image_proj, preferred_element_type=jnp.float32)
    text_raw = jnp.dot(text_feats, text_proj, preferred_element_type=jnp.float32)
    image_unit, image_norm = unit_rows(image_raw)
    text_unit, text_norm = unit_rows(text_raw)
    image_half = image_unit.astype(jnp.bfloat16)
    text_half = text_unit.astype(jnp.bfloat16)
    temp = jnp.exp(log_temp[0])
    image_unit_grad = side_grad(image_half, text_half, pair_ids, temp, bias[0], loss_grad[0])
    text_unit_grad = side_grad(text_half, image_half, pair_ids, temp, bias[0], loss_grad[0])
    image_raw_grad = ((image_unit_grad - image_unit * lax.optimization_barrier(jnp.sum(image_unit * image_unit_grad, axis=-1, keepdims=True))) / image_norm).astype(jnp.bfloat16)
    text_raw_grad = ((text_unit_grad - text_unit * lax.optimization_barrier(jnp.sum(text_unit * text_unit_grad, axis=-1, keepdims=True))) / text_norm).astype(jnp.bfloat16)
    image_grad = jnp.dot(image_raw_grad, image_proj.T, preferred_element_type=jnp.float32).astype(jnp.bfloat16)
    text_grad = jnp.dot(text_raw_grad, text_proj.T, preferred_element_type=jnp.float32).astype(jnp.bfloat16)
    weight_grads = jnp.concatenate([jnp.dot(image_feats.T, image_raw_grad, preferred_element_type=jnp.float32), jnp.dot(text_feats.T, text_raw_grad, preferred_element_type=jnp.float32)], axis=1)
    return (image_grad, text_grad, weight_grads)
```

```python
import functools

import jax
import jax.numpy as jnp
from jax import lax
from jax.experimental import pallas as pl
from jax.experimental.pallas import tpu as pltpu
from jax.sharding import PartitionSpec as P

B = 4
F32 = jnp.float32
BF16 = jnp.bfloat16


def dot(x, y, dims):
    return lax.dot_general(x, y, (dims, ((), ())), preferred_element_type=F32)


def unit_rows(raw):
    norm = jnp.sqrt(jnp.sum(raw * raw, axis=-1, keepdims=True) + 1e-06)
    return raw / norm, norm


def raw_grad_of(unit, norm, unit_grad):
    along = jnp.sum(unit * unit_grad, axis=-1, keepdims=True)
    return ((unit_grad - unit * along) / norm).astype(BF16)


def kernel(
    n, scatter,
    log_temp, bias, loss_grad, image_feats, text_feats, image_proj, text_proj, ids,
    image_grad, text_grad, weight_out,
    image_all, text_all, image_ids, text_ids, image_out, image_back, text_out, text_back,
    parts, core_in, core_sum, x_in, x_sum, z_in,
    image_sems, text_sems, image_id_sems, text_id_sems, image_back_sems, text_back_sems,
    core_sems, x_sems, z_sems,
):
    A = n // B
    rows = image_feats.shape[0]
    me = lax.axis_index("loop")
    a, b = me // B, me % B
    x, c = b // 2, b % 2
    near = [a * B + (b + k) % B for k in range(B)]
    near_back = [a * B + (b + B - k) % B for k in range(B)]
    far = [(a + k) % A * B + b for k in range(A)]
    far_back = [(a + A - k) % A * B + b for k in range(A)]
    core_peer = a * B + x * 2 + (1 - c)
    x_peer = a * B + (1 - x) * 2 + c

    def copy(src, dst, sems, where, to):
        return pltpu.make_async_remote_copy(
            src_ref=src, dst_ref=dst, send_sem=sems.at[(0,) + where], recv_sem=sems.at[(1,) + where],
            device_id={"loop": to}, device_id_type=pl.DeviceIdType.MESH,
        )

    barrier = pltpu.get_barrier_semaphore()
    for to in near[1:] + far[1:]:
        pl.semaphore_signal(
            barrier, inc=1, device_id={"loop": to}, device_id_type=pl.DeviceIdType.MESH
        )

    temp = jnp.exp(jnp.full((1, 1), log_temp[0], F32))
    bias_v = bias[0]
    scale = loss_grad[0]

    image_unit, image_norm = unit_rows(dot(image_feats[...], image_proj[...], ((1,), (0,))))
    image_all[0] = image_unit.astype(BF16)
    text_unit, text_norm = unit_rows(dot(text_feats[...], text_proj[...], ((1,), (0,))))
    text_all[0] = text_unit.astype(BF16)
    image_ids[0] = ids[...]
    text_ids[0] = ids[...]
    pl.semaphore_wait(barrier, A + B - 2)

    sent = []
    image_copies, text_copies, image_id_copies, text_id_copies = {}, {}, {}, {}
    for k in range(1, A):
        text_copies[k] = copy(text_all.at[0], text_all.at[k], text_sems, (k,), far[k])
        text_copies[k].start()
    for k in range(1, B):
        image_copies[k] = copy(image_all.at[0], image_all.at[k], image_sems, (k,), near[k])
        image_copies[k].start()
    for k in range(1, B):
        image_id_copies[k] = copy(image_ids.at[0], image_ids.at[k], image_id_sems, (k,), near[k])
        image_id_copies[k].start()
    for k in range(1, A):
        text_id_copies[k] = copy(text_ids.at[0], text_ids.at[k], text_id_sems, (k,), far[k])
        text_id_copies[k].start()
    sent += [*text_copies.values(), *image_copies.values()]
    sent += [*image_id_copies.values(), *text_id_copies.values()]

    for k in range(1, B):
        image_copies[k].wait_recv()
        image_id_copies[k].wait_recv()
    images = image_all[...].reshape(B * rows, image_all.shape[2])
    image_keys = jnp.concatenate(
        [jnp.broadcast_to(image_ids[k].astype(F32), (rows, rows)).T for k in range(B)], axis=0
    )

    image_acc = None
    text_own = None
    back = {}
    for k in [0, *range(1, A)]:
        if k:
            text_copies[k].wait_recv()
            text_id_copies[k].wait_recv()
        texts = text_all[k]
        logits = temp * dot(images, texts, ((1,), (1,))) + bias_v
        equal = (image_keys == text_ids[k].astype(F32)).astype(F32)
        coeff = (scale * (jax.nn.sigmoid(logits) - equal)).astype(BF16)
        term = dot(coeff, images, ((0,), (0,)))
        if k:
            text_out[k] = term.astype(BF16)
            back[k] = copy(text_out.at[k], text_back.at[k], text_back_sems, (k,), far_back[k])
            back[k].start()
        else:
            text_own = term
        term = dot(coeff, texts, ((1,), (0,)))
        image_acc = term if image_acc is None else image_acc + term
    sent += back.values()

    image_back_copies = {}
    for k in range(1, B):
        image_out[k] = image_acc[k * rows:(k + 1) * rows].astype(BF16)
        image_back_copies[k] = copy(
            image_out.at[k], image_back.at[k], image_back_sems, (k,), near_back[k]
        )
        image_back_copies[k].start()
    sent += image_back_copies.values()

    def reduced(own, copies, ref):
        total = own
        for k in copies:
            copies[k].wait_recv()
            total = total + ref[k].astype(F32)
        return temp * total

    sides = (
        (text_feats, text_unit, text_norm, text_own, back, text_back, text_proj, text_grad, 1),
        (image_feats, image_unit, image_norm, image_acc[:rows], image_back_copies, image_back,
         image_proj, image_grad, 0),
    )
    width = image_all.shape[2]
    raws = []
    core_copies = []
    for s, (feats, unit, norm, own, copies, ref, _, _, column) in enumerate(sides):
        raw = raw_grad_of(unit, norm, reduced(own, copies, ref))
        raws.append(raw)
        part = dot(feats[...], raw, ((0,), (0,)))
        if scatter:
            parts[s] = part.astype(BF16).reshape(parts.shape[1:])
            core_copies.append(
                copy(parts.at[s, :, :, 1 - c], core_in.at[s], core_sems, (s,), core_peer)
            )
            core_copies[s].start()
        else:
            weight_out[:, column * width:(column + 1) * width] = part

    def grad(s):
        proj, out = sides[s][6:8]
        out[...] = dot(raws[s], proj[...], ((1,), (1,))).astype(BF16)

    if not scatter:
        grad(0)
        grad(1)
    else:
        x_copies, z_copies = [], []
        for s in range(2):
            core_copies[s].wait_recv()
            core_sum[s] = (parts[s, :, :, c].astype(F32) + core_in[s].astype(F32)).astype(BF16)
            x_copies.append(copy(core_sum.at[s, :, 1 - x], x_in.at[s], x_sems, (s,), x_peer))
            x_copies[s].start()
            grad(s)
        for s in range(2):
            x_copies[s].wait_recv()
            x_sum[s] = (core_sum[s, :, x].astype(F32) + x_in[s].astype(F32)).astype(BF16)
            z_copies.append({})
            for k in range(1, A):
                z_copies[s][k] = copy(
                    x_sum.at[s, (a + k) % A], z_in.at[s, k], z_sems, (s, k), far[k]
                )
                z_copies[s][k].start()
        for s in range(2):
            total = x_sum[s, a].astype(F32)
            for k in range(1, A):
                z_copies[s][k].wait_recv()
                total = total + z_in[s, k].astype(F32)
            column = sides[s][8]
            weight_out[:, column * width:(column + 1) * width] = total
            sent += z_copies[s].values()
        sent += core_copies + x_copies
    for one in sent:
        one.wait_send()


def body(image_feats, text_feats, image_proj, text_proj, pair_ids, log_temp, bias, loss_grad):
    n = lax.axis_size("loop")
    A = n // B
    rows, depth = image_feats.shape
    width = image_proj.shape[1]
    piece = depth // n
    scatter = depth % n == 0 and piece % 16 == 0
    cut = piece if scatter else 16
    vmem = pl.BlockSpec(memory_space=pltpu.VMEM)
    smem = pl.BlockSpec(memory_space=pltpu.SMEM)
    dma = pltpu.SemaphoreType.DMA
    lead = A if scatter else 1
    image_grad, text_grad, weight = pl.pallas_call(
        functools.partial(kernel, n, scatter),
        out_shape=(
            jax.ShapeDtypeStruct((rows, depth), BF16),
            jax.ShapeDtypeStruct((rows, depth), BF16),
            jax.ShapeDtypeStruct((piece if scatter else depth, 2 * width), F32),
        ),
        in_specs=[smem] * 3 + [vmem] * 5,
        out_specs=(vmem,) * 3,
        scratch_shapes=[
            pltpu.VMEM((B, rows, width), BF16),
            pltpu.VMEM((A, rows, width), BF16),
            pltpu.VMEM((B, 1, rows), jnp.int32),
            pltpu.VMEM((A, 1, rows), jnp.int32),
            pltpu.VMEM((B, rows, width), BF16),
            pltpu.VMEM((B, rows, width), BF16),
            pltpu.VMEM((A, rows, width), BF16),
            pltpu.VMEM((A, rows, width), BF16),
            pltpu.VMEM((2, lead, 2, 2, cut, width), BF16),
            pltpu.VMEM((2, lead, 2, cut, width), BF16),
            pltpu.VMEM((2, lead, 2, cut, width), BF16),
            pltpu.VMEM((2, lead, cut, width), BF16),
            pltpu.VMEM((2, lead, cut, width), BF16),
            pltpu.VMEM((2, lead, cut, width), BF16),
            dma((2, B)),
            dma((2, A)),
            dma((2, B)),
            dma((2, A)),
            dma((2, B)),
            dma((2, A)),
            dma((2, 2)),
            dma((2, 2)),
            dma((2, 2, A)),
        ],
        compiler_params=pltpu.CompilerParams(
            collective_id=0, has_side_effects=True, vmem_limit_bytes=48 * 1024 * 1024
        ),
    )(
        log_temp, bias, loss_grad, image_feats, text_feats, image_proj, text_proj,
        pair_ids.reshape(1, rows),
    )
    if not scatter:
        weight = lax.psum_scatter(weight, "loop", scatter_dimension=0, tiled=True)
    return image_grad, text_grad, weight


def solution(mesh):
    split = P(("groups", "loop"), None)
    return jax.shard_map(
        body,
        mesh=mesh,
        in_specs=(split, split, P(), P(), P(("groups", "loop")), P(), P(), P()),
        out_specs=(split, split, split),
        check_vma=False,
    )
```

```python
import functools

import jax
import jax.numpy as jnp
from jax import lax
from jax.experimental import pallas as pl
from jax.experimental.pallas import tpu as pltpu
from jax.sharding import PartitionSpec as P

B = 4
VMEM_BYTES = 64000 * 1024
F32 = jnp.float32
BF16 = jnp.bfloat16


def dot(x, y, dims):
    return lax.dot_general(x, y, (dims, ((), ())), preferred_element_type=F32)


def unit_rows(raw):
    norm = jnp.sqrt(jnp.sum(raw * raw, axis=-1, keepdims=True) + 1e-06)
    return raw / norm, norm


def raw_grad_of(unit, norm, unit_grad):
    along = jnp.sum(unit * unit_grad, axis=-1, keepdims=True)
    return ((unit_grad - unit * along) / norm).astype(BF16)


def kernel(
    n, scatter,
    log_temp, bias, loss_grad, image_feats_hbm, text_feats_hbm, image_proj_hbm, text_proj_hbm, ids,
    image_grad_hbm, text_grad_hbm, weight_hbm,
    image_all, text_all, image_ids, text_ids, image_out, image_back, text_out, text_back,
    parts, core_in, core_sum, x_in, x_sum, z_in,
    image_feats, text_feats, image_proj, text_proj, image_turned, text_turned, load_sems,
    image_grad, text_grad, weight_out, store_sems,
    image_sems, text_sems, image_id_sems, text_id_sems, image_back_sems, text_back_sems,
    core_sems, x_sems, z_sems,
):
    A = n // B
    rows = image_feats.shape[0]
    me = lax.axis_index("loop")
    a, b = me // B, me % B
    x, c = b // 2, b % 2
    near = [a * B + (b + k) % B for k in range(B)]
    near_back = [a * B + (b + B - k) % B for k in range(B)]
    if A == 4:
        swap = [
            a,
            a + 1 - 2 * (a % 2),
            (a + 2) % 4,
            3 - a,
        ]
        far_a = far_a_back = swap
    else:
        far_a = [(a + k) % A for k in range(A)]
        far_a_back = [(a + A - k) % A for k in range(A)]
    far = [one * B + b for one in far_a]
    far_back = [one * B + b for one in far_a_back]
    far_first = [*range(2, A), 1]
    core_peer = a * B + x * 2 + (1 - c)
    x_peer = a * B + (1 - x) * 2 + c

    def copy(src, dst, sems, where, to):
        return pltpu.make_async_remote_copy(
            src_ref=src, dst_ref=dst, send_sem=sems.at[(0,) + where], recv_sem=sems.at[(1,) + where],
            device_id={"loop": to}, device_id_type=pl.DeviceIdType.MESH,
        )

    loads = [
        pltpu.make_async_copy(src, dst, load_sems.at[i])
        for i, (src, dst) in enumerate((
            (text_feats_hbm, text_feats),
            (text_proj_hbm, text_proj),
            (ids, text_ids.at[0]),
            (image_feats_hbm, image_feats),
            (image_proj_hbm, image_proj),
        ))
    ]
    for load in loads:
        load.start()
    barrier = pltpu.get_barrier_semaphore()
    for to in near[1:] + far[1:]:
        pl.semaphore_signal(
            barrier, inc=1, device_id={"loop": to}, device_id_type=pl.DeviceIdType.MESH
        )

    temp = jnp.exp(jnp.full((1, 1), log_temp[0], F32))
    bias_v = bias[0]
    scale = loss_grad[0]

    sent = []
    image_copies, text_copies, image_id_copies, text_id_copies = {}, {}, {}, {}

    for load in loads[:3]:
        load.wait()
    text_unit, text_norm = unit_rows(dot(text_feats[...], text_proj[...], ((1,), (0,))))
    text_all[0] = text_unit.astype(BF16)
    pl.semaphore_wait(barrier, A + B - 2)
    for k in far_first:
        text_copies[k] = copy(text_all.at[0], text_all.at[k], text_sems, (k,), far[k])
        text_copies[k].start()
    for load in loads[3:]:
        load.wait()
    image_unit, image_norm = unit_rows(dot(image_feats[...], image_proj[...], ((1,), (0,))))
    image_all[0] = image_unit.astype(BF16)
    for k in range(1, B):
        image_copies[k] = copy(image_all.at[0], image_all.at[k], image_sems, (k,), near[k])
        image_copies[k].start()
    for k in range(1, B):
        image_id_copies[k] = copy(text_ids.at[0], image_ids.at[k], image_id_sems, (k,), near[k])
        image_id_copies[k].start()
    for k in range(1, A):
        text_id_copies[k] = copy(text_ids.at[0], text_ids.at[k], text_id_sems, (k,), far[k])
        text_id_copies[k].start()
    sent += [*text_copies.values(), *image_copies.values()]
    sent += [*image_id_copies.values(), *text_id_copies.values()]
    image_ids[0] = text_ids[0]
    text_turned[...] = text_feats[...].T
    image_turned[...] = image_feats[...].T

    for k in range(1, B):
        image_copies[k].wait_recv()
        image_id_copies[k].wait_recv()
    images = image_all[...].reshape(B * rows, image_all.shape[2])
    image_keys = jnp.concatenate(
        [jnp.broadcast_to(image_ids[k].astype(F32), (rows, rows)).T for k in range(B)], axis=0
    )

    image_acc = None
    text_own = None
    back = {}
    for k in [0, *range(1, A)]:
        if k:
            text_copies[k].wait_recv()
            text_id_copies[k].wait_recv()
        texts = text_all[k]
        logits = temp * dot(images, texts, ((1,), (1,))) + bias_v
        equal = (image_keys == text_ids[k].astype(F32)).astype(F32)
        coeff = (scale * (jax.nn.sigmoid(logits) - equal)).astype(BF16)
        term = dot(coeff, images, ((0,), (0,)))
        if k:
            text_out[k] = term.astype(BF16)
            back[k] = copy(text_out.at[k], text_back.at[k], text_back_sems, (k,), far_back[k])
            back[k].start()
        else:
            text_own = term
        term = dot(coeff, texts, ((1,), (0,)))
        image_acc = term if image_acc is None else image_acc + term
    sent += back.values()

    image_back_copies = {}
    for k in range(1, B):
        image_out[k] = image_acc[k * rows:(k + 1) * rows].astype(BF16)
        image_back_copies[k] = copy(
            image_out.at[k], image_back.at[k], image_back_sems, (k,), near_back[k]
        )
        image_back_copies[k].start()
    sent += image_back_copies.values()

    def reduced(own, copies, ref):
        total = own
        for k in copies:
            copies[k].wait_recv()
            total = total + ref[k].astype(F32)
        return temp * total

    sides = (
        (text_turned, text_unit, text_norm, text_own, back, text_back, text_proj, text_grad, 1),
        (image_turned, image_unit, image_norm, image_acc[:rows], image_back_copies, image_back,
         image_proj, image_grad, 0),
    )
    width = image_all.shape[2]
    raws = []
    core_copies = []
    for s, (feats, unit, norm, own, copies, ref, _, _, column) in enumerate(sides):
        raw = raw_grad_of(unit, norm, reduced(own, copies, ref))
        raws.append(raw)
        part = dot(feats[...], raw, ((1,), (0,)))
        if scatter:
            parts[s] = part.astype(BF16).reshape(parts.shape[1:])
            core_copies.append(
                copy(parts.at[s, :, :, 1 - c], core_in.at[s], core_sems, (s,), core_peer)
            )
            core_copies[s].start()
        else:
            weight_out[:, column * width:(column + 1) * width] = part

    stores = [
        pltpu.make_async_copy(src, dst, store_sems.at[i])
        for i, (src, dst) in enumerate((
            (text_grad, text_grad_hbm), (image_grad, image_grad_hbm), (weight_out, weight_hbm),
        ))
    ]

    def grad(s):
        proj, out = sides[s][6:8]
        out[...] = dot(raws[s], proj[...], ((1,), (1,))).astype(BF16)
        stores[s].start()

    if not scatter:
        grad(0)
        grad(1)
    else:
        x_copies, z_copies = [], []
        for s in range(2):
            core_copies[s].wait_recv()
            core_sum[s] = (parts[s, :, :, c].astype(F32) + core_in[s].astype(F32)).astype(BF16)
            x_copies.append(copy(core_sum.at[s, :, 1 - x], x_in.at[s], x_sems, (s,), x_peer))
            x_copies[s].start()
            grad(s)
        for s in range(2):
            x_copies[s].wait_recv()
            x_sum[s] = (core_sum[s, :, x].astype(F32) + x_in[s].astype(F32)).astype(BF16)
            z_copies.append({})
            for k in far_first:
                z_copies[s][k] = copy(
                    x_sum.at[s, far_a[k]], z_in.at[s, k], z_sems, (s, k), far[k]
                )
                z_copies[s][k].start()
        for s in range(2):
            total = x_sum[s, a].astype(F32)
            for k in range(1, A):
                z_copies[s][k].wait_recv()
                total = total + z_in[s, k].astype(F32)
            column = sides[s][8]
            weight_out[:, column * width:(column + 1) * width] = total
            sent += z_copies[s].values()
        sent += core_copies + x_copies
    stores[2].start()
    for one in sent:
        one.wait_send()
    for one in stores:
        one.wait()


def store(image_in, text_in, weight_in, image_grad, text_grad, weight_out, sems):
    pairs = ((image_in, image_grad), (text_in, text_grad), (weight_in, weight_out))
    copies = [pltpu.make_async_copy(*pair, sems.at[i]) for i, pair in enumerate(pairs)]
    for one in copies:
        one.start()
    for one in copies:
        one.wait()


def body(image_feats, text_feats, image_proj, text_proj, pair_ids, log_temp, bias, loss_grad):
    n = lax.axis_size("loop")
    A = n // B
    rows, depth = image_feats.shape
    width = image_proj.shape[1]
    piece = depth // n
    scatter = depth % n == 0 and piece % 16 == 0
    cut = piece if scatter else 16
    hbm = pl.BlockSpec(memory_space=pltpu.HBM)
    smem = pl.BlockSpec(memory_space=pltpu.SMEM)
    dma = pltpu.SemaphoreType.DMA
    lead = A if scatter else 1
    image_grad, text_grad, weight = pl.pallas_call(
        functools.partial(kernel, n, scatter),
        out_shape=(
            jax.ShapeDtypeStruct((rows, depth), BF16),
            jax.ShapeDtypeStruct((rows, depth), BF16),
            jax.ShapeDtypeStruct((piece if scatter else depth, 2 * width), F32),
        ),
        in_specs=[smem] * 3 + [hbm] * 5,
        out_specs=(hbm,) * 3,
        scratch_shapes=[
            pltpu.VMEM((B, rows, width), BF16),
            pltpu.VMEM((A, rows, width), BF16),
            pltpu.VMEM((B, 1, rows), jnp.int32),
            pltpu.VMEM((A, 1, rows), jnp.int32),
            pltpu.VMEM((B, rows, width), BF16),
            pltpu.VMEM((B, rows, width), BF16),
            pltpu.VMEM((A, rows, width), BF16),
            pltpu.VMEM((A, rows, width), BF16),
            pltpu.VMEM((2, lead, 2, 2, cut, width), BF16),
            pltpu.VMEM((2, lead, 2, cut, width), BF16),
            pltpu.VMEM((2, lead, 2, cut, width), BF16),
            pltpu.VMEM((2, lead, cut, width), BF16),
            pltpu.VMEM((2, lead, cut, width), BF16),
            pltpu.VMEM((2, lead, cut, width), BF16),
            pltpu.VMEM((rows, depth), BF16),
            pltpu.VMEM((rows, depth), BF16),
            pltpu.VMEM((depth, width), BF16),
            pltpu.VMEM((depth, width), BF16),
            pltpu.VMEM((depth, rows), BF16),
            pltpu.VMEM((depth, rows), BF16),
            dma((5,)),
            pltpu.VMEM((rows, depth), BF16),
            pltpu.VMEM((rows, depth), BF16),
            pltpu.VMEM((piece if scatter else depth, 2 * width), F32),
            dma((3,)),
            dma((2, B)),
            dma((2, A)),
            dma((2, B)),
            dma((2, A)),
            dma((2, B)),
            dma((2, A)),
            dma((2, 2)),
            dma((2, 2)),
            dma((2, 2, A)),
        ],
        compiler_params=pltpu.CompilerParams(
            collective_id=0, has_side_effects=True, vmem_limit_bytes=VMEM_BYTES
        ),
    )(
        log_temp, bias, loss_grad, image_feats, text_feats, image_proj, text_proj,
        pair_ids.reshape(1, rows),
    )
    results = (image_grad, text_grad, weight)
    if scatter:
        return pl.pallas_call(
            store,
            out_shape=tuple(jax.ShapeDtypeStruct(one.shape, one.dtype) for one in results),
            in_specs=[hbm] * 3,
            out_specs=(hbm,) * 3,
            scratch_shapes=[dma((3,))],
            compiler_params=pltpu.CompilerParams(vmem_limit_bytes=VMEM_BYTES),
        )(*results)
    weight = lax.psum_scatter(weight, "loop", scatter_dimension=0, tiled=True)
    return image_grad, text_grad, weight


def solution(mesh):
    split = P(("groups", "loop"), None)
    return jax.shard_map(
        body,
        mesh=mesh,
        in_specs=(split, split, P(), P(), P(("groups", "loop")), P(), P(), P()),
        out_specs=(split, split, split),
        check_vma=False,
    )
```

```python
import functools

import jax
import jax.numpy as jnp
from jax import lax
from jax.experimental import pallas as pl
from jax.experimental.pallas import tpu as pltpu
from jax.sharding import PartitionSpec as P

B = 4
VMEM_BYTES = 64000 * 1024
F32 = jnp.float32
BF16 = jnp.bfloat16


def dot(x, y, dims):
    return lax.dot_general(x, y, (dims, ((), ())), preferred_element_type=F32)


def unit_rows(raw):
    norm = jnp.sqrt(jnp.sum(raw * raw, axis=-1, keepdims=True) + 1e-06)
    return raw / norm, norm


def raw_grad_of(unit, norm, unit_grad):
    along = jnp.sum(unit * unit_grad, axis=-1, keepdims=True)
    return ((unit_grad - unit * along) / norm).astype(BF16)


def kernel(
    n, scatter,
    log_temp, bias, loss_grad, image_feats_hbm, text_feats_hbm, image_proj_hbm, text_proj_hbm, ids,
    image_grad_hbm, text_grad_hbm, weight_hbm,
    image_all, text_all, image_ids, text_ids, image_out, image_back, text_out, text_back,
    parts, core_in, core_sum, x_in, x_sum, z_in,
    image_feats, text_feats, image_proj, text_proj, image_turned, text_turned, load_sems,
    image_grad, text_grad, weight_out, store_sems,
    image_sems, text_sems, image_id_sems, text_id_sems, image_back_sems, text_back_sems,
    core_sems, x_sems, z_sems,
):
    A = n // B
    rows = image_feats.shape[0]
    me = lax.axis_index("loop")
    a, b = me // B, me % B
    x, c = b // 2, b % 2
    near = [a * B + (b + k) % B for k in range(B)]
    near_back = [a * B + (b + B - k) % B for k in range(B)]
    if A == 4:
        swap = [
            a,
            a + 1 - 2 * (a % 2),
            (a + 2) % 4,
            3 - a,
        ]
        far_a = far_a_back = swap
    else:
        far_a = [(a + k) % A for k in range(A)]
        far_a_back = [(a + A - k) % A for k in range(A)]
    far = [one * B + b for one in far_a]
    far_back = [one * B + b for one in far_a_back]
    far_first = [*range(2, A), 1]
    core_peer = a * B + x * 2 + (1 - c)
    x_peer = a * B + (1 - x) * 2 + c

    def copy(src, dst, sems, where, to):
        return pltpu.make_async_remote_copy(
            src_ref=src, dst_ref=dst, send_sem=sems.at[(0,) + where], recv_sem=sems.at[(1,) + where],
            device_id={"loop": to}, device_id_type=pl.DeviceIdType.MESH,
        )

    loads = [
        pltpu.make_async_copy(src, dst, load_sems.at[i])
        for i, (src, dst) in enumerate((
            (text_feats_hbm, text_feats),
            (text_proj_hbm, text_proj),
            (ids, text_ids.at[0]),
            (image_feats_hbm, image_feats),
            (image_proj_hbm, image_proj),
        ))
    ]
    for load in loads:
        load.start()
    barrier = pltpu.get_barrier_semaphore()
    for to in near[1:] + far[1:]:
        pl.semaphore_signal(
            barrier, inc=1, device_id={"loop": to}, device_id_type=pl.DeviceIdType.MESH
        )

    temp = jnp.exp(jnp.full((1, 1), log_temp[0], F32))
    bias_v = bias[0]
    scale = loss_grad[0]

    sent = []
    image_copies, text_copies, image_id_copies, text_id_copies = {}, {}, {}, {}

    for load in loads[:3]:
        load.wait()
    text_unit, text_norm = unit_rows(dot(text_feats[...], text_proj[...], ((1,), (0,))))
    text_all[0] = text_unit.astype(BF16)
    pl.semaphore_wait(barrier, A + B - 2)
    for k in far_first:
        text_copies[k] = copy(text_all.at[0], text_all.at[k], text_sems, (k,), far[k])
        text_copies[k].start()
    for load in loads[3:]:
        load.wait()
    image_unit, image_norm = unit_rows(dot(image_feats[...], image_proj[...], ((1,), (0,))))
    image_all[0] = image_unit.astype(BF16)
    for k in range(1, B):
        image_copies[k] = copy(image_all.at[0], image_all.at[k], image_sems, (k,), near[k])
        image_copies[k].start()
    for k in range(1, B):
        image_id_copies[k] = copy(text_ids.at[0], image_ids.at[k], image_id_sems, (k,), near[k])
        image_id_copies[k].start()
    for k in range(1, A):
        text_id_copies[k] = copy(text_ids.at[0], text_ids.at[k], text_id_sems, (k,), far[k])
        text_id_copies[k].start()
    sent += [*text_copies.values(), *image_copies.values()]
    sent += [*image_id_copies.values(), *text_id_copies.values()]
    image_ids[0] = text_ids[0]
    text_turned[...] = text_feats[...].T
    image_turned[...] = image_feats[...].T

    for k in range(1, B):
        image_copies[k].wait_recv()
        image_id_copies[k].wait_recv()
    images = image_all[...].reshape(B * rows, image_all.shape[2])
    image_keys = jnp.concatenate(
        [jnp.broadcast_to(image_ids[k].astype(F32), (rows, rows)).T for k in range(B)], axis=0
    )

    image_acc = None
    text_own = None
    back = {}
    for k in [0, *range(1, A)]:
        if k:
            text_copies[k].wait_recv()
            text_id_copies[k].wait_recv()
        texts = text_all[k]
        logits = temp * dot(images, texts, ((1,), (1,))) + bias_v
        equal = (image_keys == text_ids[k].astype(F32)).astype(F32)
        coeff = (scale * (jax.nn.sigmoid(logits) - equal)).astype(BF16)
        term = dot(coeff, images, ((0,), (0,)))
        if k:
            text_out[k] = term.astype(BF16)
            back[k] = copy(text_out.at[k], text_back.at[k], text_back_sems, (k,), far_back[k])
            back[k].start()
        else:
            text_own = term
        term = dot(coeff, texts, ((1,), (0,)))
        image_acc = term if image_acc is None else image_acc + term
    sent += back.values()

    image_back_copies = {}
    for k in range(1, B):
        image_out[k] = image_acc[k * rows:(k + 1) * rows].astype(BF16)
        image_back_copies[k] = copy(
            image_out.at[k], image_back.at[k], image_back_sems, (k,), near_back[k]
        )
        image_back_copies[k].start()
    sent += image_back_copies.values()

    def reduced(own, copies, ref):
        total = own
        for k in copies:
            copies[k].wait_recv()
            total = total + ref[k].astype(F32)
        return temp * total

    sides = (
        (text_turned, text_unit, text_norm, text_own, back, text_back, text_proj, text_grad, 1),
        (image_turned, image_unit, image_norm, image_acc[:rows], image_back_copies, image_back,
         image_proj, image_grad, 0),
    )
    width = image_all.shape[2]
    raws = []
    core_copies = []
    for s, (feats, unit, norm, own, copies, ref, _, _, column) in enumerate(sides):
        raw = raw_grad_of(unit, norm, reduced(own, copies, ref))
        raws.append(raw)
        part = dot(feats[...], raw, ((1,), (0,)))
        if scatter:
            parts[s] = part.astype(BF16).reshape(parts.shape[1:])
            core_copies.append(
                copy(parts.at[s, :, :, 1 - c], core_in.at[s], core_sems, (s,), core_peer)
            )
            core_copies[s].start()
        else:
            weight_out[:, column * width:(column + 1) * width] = part

    stores = [
        pltpu.make_async_copy(src, dst, store_sems.at[i])
        for i, (src, dst) in enumerate((
            (text_grad, text_grad_hbm), (image_grad, image_grad_hbm), (weight_out, weight_hbm),
        ))
    ]

    def grad(s):
        proj, out = sides[s][6:8]
        out[...] = dot(raws[s], proj[...], ((1,), (1,))).astype(BF16)
        stores[s].start()

    if not scatter:
        grad(0)
        grad(1)
    else:
        x_copies, z_copies = [], []
        for s in range(2):
            core_copies[s].wait_recv()
            core_sum[s] = (parts[s, :, :, c].astype(F32) + core_in[s].astype(F32)).astype(BF16)
            x_copies.append(copy(core_sum.at[s, :, 1 - x], x_in.at[s], x_sems, (s,), x_peer))
            x_copies[s].start()
            grad(s)
        for s in range(2):
            x_copies[s].wait_recv()
            x_sum[s] = (core_sum[s, :, x].astype(F32) + x_in[s].astype(F32)).astype(BF16)
            z_copies.append({})
            for k in far_first:
                z_copies[s][k] = copy(
                    x_sum.at[s, far_a[k]], z_in.at[s, k], z_sems, (s, k), far[k]
                )
                z_copies[s][k].start()
        for s in range(2):
            total = x_sum[s, a].astype(F32)
            for k in range(1, A):
                z_copies[s][k].wait_recv()
                total = total + z_in[s, k].astype(F32)
            column = sides[s][8]
            weight_out[:, column * width:(column + 1) * width] = total
            sent += z_copies[s].values()
        sent += core_copies + x_copies
    stores[2].start()
    for one in sent:
        one.wait_send()
    for one in stores:
        one.wait()


def store(
    image_in, text_in, weight_in, image_grad, text_grad, weight_out, image_buf, text_buf, weight_buf, sems
):
    sources, targets = (image_in, text_in, weight_in), (image_grad, text_grad, weight_out)
    buffers = (image_buf, text_buf, weight_buf)
    loads = [pltpu.make_async_copy(sources[i], buffers[i], sems.at[0, i]) for i in range(3)]
    stores = [pltpu.make_async_copy(buffers[i], targets[i], sems.at[1, i]) for i in range(3)]
    for one in loads:
        one.start()
    for load, one in zip(loads, stores):
        load.wait()
        one.start()
    for one in stores:
        one.wait()


def body(image_feats, text_feats, image_proj, text_proj, pair_ids, log_temp, bias, loss_grad):
    n = lax.axis_size("loop")
    A = n // B
    rows, depth = image_feats.shape
    width = image_proj.shape[1]
    piece = depth // n
    scatter = depth % n == 0 and piece % 16 == 0
    cut = piece if scatter else 16
    hbm = pl.BlockSpec(memory_space=pltpu.HBM)
    smem = pl.BlockSpec(memory_space=pltpu.SMEM)
    dma = pltpu.SemaphoreType.DMA
    lead = A if scatter else 1
    image_grad, text_grad, weight = pl.pallas_call(
        functools.partial(kernel, n, scatter),
        out_shape=(
            jax.ShapeDtypeStruct((rows, depth), BF16),
            jax.ShapeDtypeStruct((rows, depth), BF16),
            jax.ShapeDtypeStruct((piece if scatter else depth, 2 * width), F32),
        ),
        in_specs=[smem] * 3 + [hbm] * 5,
        out_specs=(hbm,) * 3,
        scratch_shapes=[
            pltpu.VMEM((B, rows, width), BF16),
            pltpu.VMEM((A, rows, width), BF16),
            pltpu.VMEM((B, 1, rows), jnp.int32),
            pltpu.VMEM((A, 1, rows), jnp.int32),
            pltpu.VMEM((B, rows, width), BF16),
            pltpu.VMEM((B, rows, width), BF16),
            pltpu.VMEM((A, rows, width), BF16),
            pltpu.VMEM((A, rows, width), BF16),
            pltpu.VMEM((2, lead, 2, 2, cut, width), BF16),
            pltpu.VMEM((2, lead, 2, cut, width), BF16),
            pltpu.VMEM((2, lead, 2, cut, width), BF16),
            pltpu.VMEM((2, lead, cut, width), BF16),
            pltpu.VMEM((2, lead, cut, width), BF16),
            pltpu.VMEM((2, lead, cut, width), BF16),
            pltpu.VMEM((rows, depth), BF16),
            pltpu.VMEM((rows, depth), BF16),
            pltpu.VMEM((depth, width), BF16),
            pltpu.VMEM((depth, width), BF16),
            pltpu.VMEM((depth, rows), BF16),
            pltpu.VMEM((depth, rows), BF16),
            dma((5,)),
            pltpu.VMEM((rows, depth), BF16),
            pltpu.VMEM((rows, depth), BF16),
            pltpu.VMEM((piece if scatter else depth, 2 * width), F32),
            dma((3,)),
            dma((2, B)),
            dma((2, A)),
            dma((2, B)),
            dma((2, A)),
            dma((2, B)),
            dma((2, A)),
            dma((2, 2)),
            dma((2, 2)),
            dma((2, 2, A)),
        ],
        compiler_params=pltpu.CompilerParams(
            collective_id=0, has_side_effects=True, vmem_limit_bytes=VMEM_BYTES
        ),
    )(
        log_temp, bias, loss_grad, image_feats, text_feats, image_proj, text_proj,
        pair_ids.reshape(1, rows),
    )
    results = (image_grad, text_grad, weight)
    if scatter:
        return pl.pallas_call(
            store,
            out_shape=tuple(jax.ShapeDtypeStruct(one.shape, one.dtype) for one in results),
            in_specs=[hbm] * 3,
            out_specs=(hbm,) * 3,
            scratch_shapes=[pltpu.VMEM(one.shape, one.dtype) for one in results] + [dma((2, 3))],
            compiler_params=pltpu.CompilerParams(vmem_limit_bytes=VMEM_BYTES),
        )(*results)
    weight = lax.psum_scatter(weight, "loop", scatter_dimension=0, tiled=True)
    return image_grad, text_grad, weight


def solution(mesh):
    split = P(("groups", "loop"), None)
    return jax.shard_map(
        body,
        mesh=mesh,
        in_specs=(split, split, P(), P(), P(("groups", "loop")), P(), P(), P()),
        out_specs=(split, split, split),
        check_vma=False,
    )
```

```python
import functools

import jax
import jax.numpy as jnp
from jax import lax
from jax.experimental import pallas as pl
from jax.experimental.pallas import tpu as pltpu
from jax.sharding import PartitionSpec as P

B = 4
VMEM_BYTES = 64000 * 1024
F32 = jnp.float32
BF16 = jnp.bfloat16


def dot(x, y, dims):
    return lax.dot_general(x, y, (dims, ((), ())), preferred_element_type=F32)


def unit_rows(raw):
    norm = jnp.sqrt(jnp.sum(raw * raw, axis=-1, keepdims=True) + 1e-06)
    return raw / norm, norm


def raw_grad_of(unit, norm, unit_grad):
    along = jnp.sum(unit * unit_grad, axis=-1, keepdims=True)
    return ((unit_grad - unit * along) / norm).astype(BF16)


def kernel(
    n, scatter,
    log_temp, bias, loss_grad, image_feats_hbm, text_feats_hbm, image_proj_hbm, text_proj_hbm, ids,
    image_grad_hbm, text_grad_hbm, weight_hbm,
    image_all, text_all, image_ids, text_ids, image_out, image_back, text_out, text_back,
    parts, core_in, core_sum, x_in, x_sum, z_in,
    image_feats, text_feats, image_proj, text_proj, image_turned, text_turned, load_sems,
    image_grad, text_grad, weight_out, store_sems,
    image_sems, text_sems, image_id_sems, text_id_sems, image_back_sems, text_back_sems,
    core_sems, x_sems, z_sems,
):
    A = n // B
    rows = image_feats.shape[0]
    me = lax.axis_index("loop")
    a, b = me // B, me % B
    x, c = b // 2, b % 2
    near = [a * B + (b + k) % B for k in range(B)]
    near_back = [a * B + (b + B - k) % B for k in range(B)]
    if A == 4:
        swap = [
            a,
            a + 1 - 2 * (a % 2),
            (a + 2) % 4,
            3 - a,
        ]
        far_a = far_a_back = swap
    else:
        far_a = [(a + k) % A for k in range(A)]
        far_a_back = [(a + A - k) % A for k in range(A)]
    far = [one * B + b for one in far_a]
    far_back = [one * B + b for one in far_a_back]
    far_first = [*range(2, A), 1]
    core_peer = a * B + x * 2 + (1 - c)
    x_peer = a * B + (1 - x) * 2 + c

    def copy(src, dst, sems, where, to):
        return pltpu.make_async_remote_copy(
            src_ref=src, dst_ref=dst, send_sem=sems.at[(0,) + where], recv_sem=sems.at[(1,) + where],
            device_id={"loop": to}, device_id_type=pl.DeviceIdType.MESH,
        )

    loads = [
        pltpu.make_async_copy(src, dst, load_sems.at[i])
        for i, (src, dst) in enumerate((
            (text_feats_hbm, text_feats),
            (text_proj_hbm, text_proj),
            (ids, text_ids.at[0]),
            (image_feats_hbm, image_feats),
            (image_proj_hbm, image_proj),
        ))
    ]
    for load in loads:
        load.start()
    barrier = pltpu.get_barrier_semaphore()
    for to in near[1:] + far[1:]:
        pl.semaphore_signal(
            barrier, inc=1, device_id={"loop": to}, device_id_type=pl.DeviceIdType.MESH
        )

    temp = jnp.exp(jnp.full((1, 1), log_temp[0], F32))
    bias_v = bias[0]
    scale = loss_grad[0]

    sent = []
    image_copies, text_copies, image_id_copies, text_id_copies = {}, {}, {}, {}

    for load in loads[:3]:
        load.wait()
    text_unit, text_norm = unit_rows(dot(text_feats[...], text_proj[...], ((1,), (0,))))
    text_all[0] = text_unit.astype(BF16)
    pl.semaphore_wait(barrier, A + B - 2)
    for k in far_first:
        if A == 4 and k == 3:
            continue
        text_copies[k] = copy(text_all.at[0], text_all.at[k], text_sems, (k,), far[k])
        text_copies[k].start()
    for load in loads[3:]:
        load.wait()
    image_unit, image_norm = unit_rows(dot(image_feats[...], image_proj[...], ((1,), (0,))))
    image_all[0] = image_unit.astype(BF16)
    for k in range(1, B):
        image_copies[k] = copy(image_all.at[0], image_all.at[k], image_sems, (k,), near[k])
        image_copies[k].start()
    for k in range(1, B):
        image_id_copies[k] = copy(text_ids.at[0], image_ids.at[k], image_id_sems, (k,), near[k])
        image_id_copies[k].start()
    for k in range(1, A):
        text_id_copies[k] = copy(text_ids.at[0], text_ids.at[k], text_id_sems, (k,), far[k])
        text_id_copies[k].start()
    sent += [*image_copies.values()]
    sent += [*image_id_copies.values(), *text_id_copies.values()]
    image_ids[0] = text_ids[0]
    text_turned[...] = text_feats[...].T
    image_turned[...] = image_feats[...].T

    for k in range(1, B):
        image_copies[k].wait_recv()
        image_id_copies[k].wait_recv()
    images = image_all[...].reshape(B * rows, image_all.shape[2])
    image_keys = jnp.concatenate(
        [jnp.broadcast_to(image_ids[k].astype(F32), (rows, rows)).T for k in range(B)], axis=0
    )

    image_acc = None
    text_own = None
    back = {}
    for k in [0, *range(1, A)]:
        if A == 4 and k == 1:
            text_copies[2].wait_recv()
            text_copies[3] = copy(text_all.at[2], text_all.at[3], text_sems, (3,), far[1])
            text_copies[3].start()
        if k:
            if A != 4 or k != 2:
                text_copies[k].wait_recv()
            text_id_copies[k].wait_recv()
        texts = text_all[k]
        logits = temp * dot(images, texts, ((1,), (1,))) + bias_v
        equal = (image_keys == text_ids[k].astype(F32)).astype(F32)
        coeff = (scale * (jax.nn.sigmoid(logits) - equal)).astype(BF16)
        term = dot(coeff, images, ((0,), (0,)))
        if A == 4 and k == 2:
            crossing = term
        elif k:
            text_out[k] = term.astype(BF16)
            back[k] = copy(text_out.at[k], text_back.at[k], text_back_sems, (k,), far[1] if A == 4 else far_back[k])
            back[k].start()
        else:
            text_own = term
        term = dot(coeff, texts, ((1,), (0,)))
        image_acc = term if image_acc is None else image_acc + term
    sent += text_copies.values()

    image_back_copies = {}
    for k in range(1, B):
        image_out[k] = image_acc[k * rows:(k + 1) * rows].astype(BF16)
        image_back_copies[k] = copy(
            image_out.at[k], image_back.at[k], image_back_sems, (k,), near_back[k]
        )
        image_back_copies[k].start()
    sent += image_back_copies.values()
    sent += back.values()
    if A == 4:
        back[3].wait_recv()
        text_out[2] = (crossing + text_back[3].astype(F32)).astype(BF16)
        back[2] = copy(text_out.at[2], text_back.at[2], text_back_sems, (2,), far[2])
        back[2].start()
        sent.append(back[2])
        del back[3]

    def reduced(own, copies, ref):
        total = own
        for k in copies:
            copies[k].wait_recv()
            total = total + ref[k].astype(F32)
        return temp * total

    sides = (
        (text_turned, text_unit, text_norm, text_own, back, text_back, text_proj, text_grad, 1),
        (image_turned, image_unit, image_norm, image_acc[:rows], image_back_copies, image_back,
         image_proj, image_grad, 0),
    )
    width = image_all.shape[2]
    raws = []
    core_copies = []
    for s, (feats, unit, norm, own, copies, ref, _, _, column) in enumerate(sides):
        raw = raw_grad_of(unit, norm, reduced(own, copies, ref))
        raws.append(raw)
        part = dot(feats[...], raw, ((1,), (0,)))
        if scatter:
            parts[s] = part.astype(BF16).reshape(parts.shape[1:])
            core_copies.append(
                copy(parts.at[s, :, :, 1 - c], core_in.at[s], core_sems, (s,), core_peer)
            )
            core_copies[s].start()
        else:
            weight_out[:, column * width:(column + 1) * width] = part

    stores = [
        pltpu.make_async_copy(src, dst, store_sems.at[i])
        for i, (src, dst) in enumerate((
            (text_grad, text_grad_hbm), (image_grad, image_grad_hbm), (weight_out, weight_hbm),
        ))
    ]

    def grad(s):
        proj, out = sides[s][6:8]
        out[...] = dot(raws[s], proj[...], ((1,), (1,))).astype(BF16)
        stores[s].start()

    if not scatter:
        grad(0)
        grad(1)
    else:
        x_copies, z_copies = [], []
        for s in range(2):
            core_copies[s].wait_recv()
            core_sum[s] = (parts[s, :, :, c].astype(F32) + core_in[s].astype(F32)).astype(BF16)
            x_copies.append(copy(core_sum.at[s, :, 1 - x], x_in.at[s], x_sems, (s,), x_peer))
            x_copies[s].start()
            grad(s)
        for s in range(2):
            x_copies[s].wait_recv()
            x_sum[s] = (core_sum[s, :, x].astype(F32) + x_in[s].astype(F32)).astype(BF16)
            z_copies.append({})
            for k in far_first:
                z_copies[s][k] = copy(
                    x_sum.at[s, far_a[k]], z_in.at[s, k], z_sems, (s, k), far[k]
                )
                z_copies[s][k].start()
        for s in range(2):
            total = x_sum[s, a].astype(F32)
            for k in range(1, A):
                z_copies[s][k].wait_recv()
                total = total + z_in[s, k].astype(F32)
            column = sides[s][8]
            weight_out[:, column * width:(column + 1) * width] = total
            sent += z_copies[s].values()
        sent += core_copies + x_copies
    stores[2].start()
    for one in sent:
        one.wait_send()
    for one in stores:
        one.wait()


def store(
    image_in, text_in, weight_in, image_grad, text_grad, weight_out, image_buf, text_buf, weight_buf, sems
):
    sources, targets = (image_in, text_in, weight_in), (image_grad, text_grad, weight_out)
    buffers = (image_buf, text_buf, weight_buf)
    loads = [pltpu.make_async_copy(sources[i], buffers[i], sems.at[0, i]) for i in range(3)]
    stores = [pltpu.make_async_copy(buffers[i], targets[i], sems.at[1, i]) for i in range(3)]
    for one in loads:
        one.start()
    for load, one in zip(loads, stores):
        load.wait()
        one.start()
    for one in stores:
        one.wait()


def body(image_feats, text_feats, image_proj, text_proj, pair_ids, log_temp, bias, loss_grad):
    n = lax.axis_size("loop")
    A = n // B
    rows, depth = image_feats.shape
    width = image_proj.shape[1]
    piece = depth // n
    scatter = depth % n == 0 and piece % 16 == 0
    cut = piece if scatter else 16
    hbm = pl.BlockSpec(memory_space=pltpu.HBM)
    smem = pl.BlockSpec(memory_space=pltpu.SMEM)
    dma = pltpu.SemaphoreType.DMA
    lead = A if scatter else 1
    image_grad, text_grad, weight = pl.pallas_call(
        functools.partial(kernel, n, scatter),
        out_shape=(
            jax.ShapeDtypeStruct((rows, depth), BF16),
            jax.ShapeDtypeStruct((rows, depth), BF16),
            jax.ShapeDtypeStruct((piece if scatter else depth, 2 * width), F32),
        ),
        in_specs=[smem] * 3 + [hbm] * 5,
        out_specs=(hbm,) * 3,
        scratch_shapes=[
            pltpu.VMEM((B, rows, width), BF16),
            pltpu.VMEM((A, rows, width), BF16),
            pltpu.VMEM((B, 1, rows), jnp.int32),
            pltpu.VMEM((A, 1, rows), jnp.int32),
            pltpu.VMEM((B, rows, width), BF16),
            pltpu.VMEM((B, rows, width), BF16),
            pltpu.VMEM((A, rows, width), BF16),
            pltpu.VMEM((A, rows, width), BF16),
            pltpu.VMEM((2, lead, 2, 2, cut, width), BF16),
            pltpu.VMEM((2, lead, 2, cut, width), BF16),
            pltpu.VMEM((2, lead, 2, cut, width), BF16),
            pltpu.VMEM((2, lead, cut, width), BF16),
            pltpu.VMEM((2, lead, cut, width), BF16),
            pltpu.VMEM((2, lead, cut, width), BF16),
            pltpu.VMEM((rows, depth), BF16),
            pltpu.VMEM((rows, depth), BF16),
            pltpu.VMEM((depth, width), BF16),
            pltpu.VMEM((depth, width), BF16),
            pltpu.VMEM((depth, rows), BF16),
            pltpu.VMEM((depth, rows), BF16),
            dma((5,)),
            pltpu.VMEM((rows, depth), BF16),
            pltpu.VMEM((rows, depth), BF16),
            pltpu.VMEM((piece if scatter else depth, 2 * width), F32),
            dma((3,)),
            dma((2, B)),
            dma((2, A)),
            dma((2, B)),
            dma((2, A)),
            dma((2, B)),
            dma((2, A)),
            dma((2, 2)),
            dma((2, 2)),
            dma((2, 2, A)),
        ],
        compiler_params=pltpu.CompilerParams(
            collective_id=0, has_side_effects=True, vmem_limit_bytes=VMEM_BYTES
        ),
    )(
        log_temp, bias, loss_grad, image_feats, text_feats, image_proj, text_proj,
        pair_ids.reshape(1, rows),
    )
    results = (image_grad, text_grad, weight)
    if scatter:
        return pl.pallas_call(
            store,
            out_shape=tuple(jax.ShapeDtypeStruct(one.shape, one.dtype) for one in results),
            in_specs=[hbm] * 3,
            out_specs=(hbm,) * 3,
            scratch_shapes=[pltpu.VMEM(one.shape, one.dtype) for one in results] + [dma((2, 3))],
            compiler_params=pltpu.CompilerParams(vmem_limit_bytes=VMEM_BYTES),
        )(*results)
    weight = lax.psum_scatter(weight, "loop", scatter_dimension=0, tiled=True)
    return image_grad, text_grad, weight


def solution(mesh):
    split = P(("groups", "loop"), None)
    return jax.shard_map(
        body,
        mesh=mesh,
        in_specs=(split, split, P(), P(), P(("groups", "loop")), P(), P(), P()),
        out_specs=(split, split, split),
        check_vma=False,
    )
```
